256 devices in a mesh: dom: 64 (over x, z, core), loop: 4 (over y).
Axes of the slice: x: 4, y: 4, z: 8, core: 2. Of those that a mesh axis runs over, the one named last changes fastest.
Arguments:
- node_rows: bfloat16 [131072, 512], P(('dom', 'loop')), may hold values from -24 to 24
- w_dst: bfloat16 [512, 512], replicated, may hold values from -0.25 to 0.25
- w_src: bfloat16 [512, 512], replicated, may hold values from -0.25 to 0.25
- w_val: bfloat16 [512, 512], replicated, may hold values from -0.25 to 0.25
- w_query: bfloat16 [512, 512], replicated, may hold values from -0.25 to 0.25
- w_key: bfloat16 [512, 512], replicated, may hold values from -0.25 to 0.25
- w_value: bfloat16 [512, 512], replicated, may hold values from -0.25 to 0.25
- w_out: bfloat16 [512, 512], replicated, may hold values from -0.25 to 0.25
- norm_gain: float32 [512], replicated, may hold values from 0.5 to 1.5
- send_rows: int32 [64, 4, 64, 32], P('dom', 'loop'), may hold values from 0 to 511
- dst_rows: int32 [64, 4, 64, 32], P('dom', 'loop'), may hold values from 0 to 511
- counts: int32 [64, 4, 64], P('dom', 'loop'), may hold values from 1 to 32, as said below
- batch_ids: int32 [64, 2048], P('dom', 'loop'), may hold values from 0 to 1, never falling along the last dimension, each value on 1 to 1536 neighbouring positions
Outputs:
- layer_out: bfloat16 [131072, 512], P(('dom', 'loop'))
The draws below stay inside these ranges and needn't reach their ends.
Inputs may be any that keep to these rules, and one draw needn't show every extreme that they name: `counts`: every device receives a full block of 32 live slots from some partition. `batch_ids`: each partition's nodes form two contiguous batches, each of 512 to 1536 nodes.
All inputs are finite; a program needn't handle non-finite values.
Results may differ from the reference program's by a relative error of at most 0.012.
The reference program's roundings to bfloat16 on the way (of `mixed`) count: a program that leaves them out, or rounds other values in their place, can miss the bound.
Values may be sent and summed in bfloat16 or wider, within the bound.
A program may use at most 128 MiB of HBM per device.

```python
import math
import jax
import jax.numpy as jnp
import numpy as np
from jax import lax

D = 512
HEADS = 8
HEAD_DIM = 64
ROWS = 512
CAP = 32
PARTS_SIZE = 64
LOOPS = 4
GROUP = 2048
NODES = 131072


def draw_node_rows(key, part):
    key = jax.random.fold_in(key, 7)
    first = jax.random.fold_in(key, 0)
    values = jax.random.normal(first, (NODES, D), jnp.float32)
    return jnp.clip(values, -24.0, 24.0).astype(jnp.bfloat16)


def draw_counts(key, part):
    key = jax.random.fold_in(key, 5)
    first, second = jax.random.split(key)
    base = jax.random.randint(first, (PARTS_SIZE, LOOPS, PARTS_SIZE), 1, CAP + 1)
    position = jax.random.randint(second, (PARTS_SIZE, LOOPS, 1), 0, PARTS_SIZE)
    column = jnp.arange(PARTS_SIZE, dtype=jnp.int32)[None, None, :]
    return jnp.where(column == position, CAP, base).astype(jnp.int32)


def set_ends(result, own_key, least, largest):
    dims = result.shape
    index_at = [jax.random.randint(jax.random.fold_in(own_key, axis), (), 0, dims[axis]) for axis in range(len(dims))]
    result = result.at[tuple(index_at)].set(least)
    longest = dims.index(max(dims))
    index_at[longest] = (index_at[longest] + 1) % dims[longest]
    return result.at[tuple(index_at)].set(largest)


def split_up(amount, total, bound, lean):
    portions = [(1 << 20) // math.isqrt(standing ** lean) + 1 for standing in range(2, amount + 1)]
    spare, holding = total - bound - (amount - 1), [1] * (amount - 1)
    while spare > 0:
        movable = [i for i in range(amount - 1) if holding[i] < bound]
        whole, budget = sum([portions[i] for i in movable]), spare
        for i in movable:
            addition = min(bound - holding[i], max(1, budget * portions[i] // whole), spare)
            holding[i] = holding[i] + addition
            spare = spare - addition
    return np.array([bound] + holding)


def ragged_sizes(stream_key, count, total, reach, slope):
    if count == 2:
        one = jax.random.randint(stream_key, (), max(1, total - reach), min(reach, total - 1) + 1)
        return jnp.stack([one, total - one])
    tallies = jnp.asarray(split_up(count, total, reach, slope), jnp.int32)
    pairs = (count - 1) // 2
    giver, receiver = tallies[1:1 + 2 * pairs:2], tallies[2:2 + 2 * pairs:2]
    slack = jnp.minimum(giver - 1, reach - receiver)
    passed = jax.random.randint(jax.random.fold_in(stream_key, 1), (pairs,), 0, 1 << 20) % (slack + 1)
    tallies = tallies.at[1:1 + 2 * pairs:2].set(giver - passed).at[2:2 + 2 * pairs:2].set(receiver + passed)
    return tallies[jax.random.permutation(jax.random.fold_in(stream_key, 2), count)]


def bell_draw(own_key, extent, deviation, limit, held_as=jnp.bfloat16):
    result = deviation * jax.random.normal(own_key, extent, jnp.float32)
    return jnp.clip(result, min=-limit, max=limit).astype(held_as)


def setup_inputs(seed: int = 0) -> dict:
    seeds = jax.random.split(jax.random.key(seed), 14)
    return {
        "node_rows": draw_node_rows(jax.random.fold_in(seeds[13], 71), 0),
        "w_dst": bell_draw(seeds[1], (D, D), D ** -0.5, 0.25),
        "w_src": bell_draw(seeds[2], (D, D), D ** -0.5, 0.25),
        "w_val": bell_draw(seeds[3], (D, D), D ** -0.5, 0.25),
        "w_query": bell_draw(seeds[4], (D, D), D ** -0.5, 0.25),
        "w_key": bell_draw(seeds[5], (D, D), D ** -0.5, 0.25),
        "w_value": bell_draw(seeds[6], (D, D), D ** -0.5, 0.25),
        "w_out": bell_draw(seeds[7], (D, D), D ** -0.5, 0.25),
        "norm_gain": jnp.clip(1.0 + 0.1 * jax.random.normal(seeds[8], (D,), jnp.float32), 0.5, 1.5),
        "send_rows": set_ends(jax.random.randint(seeds[9], (PARTS_SIZE, LOOPS, PARTS_SIZE, CAP), 0, ROWS), jax.random.fold_in(seeds[9], 1), 0, ROWS - 1).astype(jnp.int32),
        "dst_rows": set_ends(jax.random.randint(seeds[10], (PARTS_SIZE, LOOPS, PARTS_SIZE, CAP), 0, ROWS), jax.random.fold_in(seeds[10], 1), 0, ROWS - 1).astype(jnp.int32),
        "counts": draw_counts(jax.random.fold_in(seeds[13], 71), 0),
        "batch_ids": jax.vmap(lambda own: jnp.searchsorted(jnp.cumsum(ragged_sizes(own, 2, GROUP, 3 * ROWS, 0)), jnp.arange(GROUP), side="right"))(jax.random.split(seeds[12], PARTS_SIZE)).reshape((PARTS_SIZE, GROUP)).astype(jnp.int32),
    }


def reference(node_rows, w_dst, w_src, w_val, w_query, w_key, w_value, w_out, norm_gain, send_rows, dst_rows, counts, batch_ids):
    dst_term = jnp.dot(node_rows, w_dst, preferred_element_type=jnp.float32)
    src_term = jnp.dot(node_rows, w_src, preferred_element_type=jnp.float32).astype(jnp.bfloat16)
    val_term = jnp.dot(node_rows, w_val, preferred_element_type=jnp.float32).astype(jnp.bfloat16)
    slab_dst = dst_term.reshape(PARTS_SIZE, LOOPS, ROWS, D)
    slab_src = src_term.reshape(PARTS_SIZE, LOOPS, ROWS, D)
    slab_val = val_term.reshape(PARTS_SIZE, LOOPS, ROWS, D)
    sender_rows = jnp.transpose(send_rows, (2, 1, 0, 3))

    def device_messages(device):
        part_idx = device // LOOPS
        loop_idx = device % LOOPS
        chosen = sender_rows[part_idx, loop_idx][:, :, None]
        edge_src = jnp.take_along_axis(slab_src[:, loop_idx], chosen, axis=1).reshape(-1, D).astype(jnp.float32)
        edge_val = jnp.take_along_axis(slab_val[:, loop_idx], chosen, axis=1).reshape(-1, D).astype(jnp.float32)
        targets = dst_rows[part_idx, loop_idx].reshape(-1)
        live_slot = (jnp.arange(CAP, dtype=jnp.int32)[None, :] < counts[part_idx, loop_idx][:, None]).reshape(-1)
        gates = jax.nn.sigmoid(jnp.take(slab_dst[part_idx, loop_idx], targets, axis=0) + edge_src)
        gates = jnp.where(live_slot[:, None], gates, 0.0)
        numerator = jax.ops.segment_sum(gates * edge_val, targets, num_segments=ROWS)
        denominator = jax.ops.segment_sum(gates, targets, num_segments=ROWS)
        return numerator / (1.0 + denominator)
    aggregated = lax.map(device_messages, jnp.arange(PARTS_SIZE * LOOPS, dtype=jnp.int32)).reshape(NODES, D)
    queries = jnp.dot(node_rows, w_query, preferred_element_type=jnp.float32).astype(jnp.bfloat16).reshape(PARTS_SIZE, GROUP, HEADS, HEAD_DIM)
    keys = jnp.dot(node_rows, w_key, preferred_element_type=jnp.float32).astype(jnp.bfloat16).reshape(PARTS_SIZE, GROUP, HEADS, HEAD_DIM)
    values = jnp.dot(node_rows, w_value, preferred_element_type=jnp.float32).astype(jnp.bfloat16).reshape(PARTS_SIZE, GROUP, HEADS, HEAD_DIM)
    scale_factor = 1.0 / math.sqrt(HEAD_DIM)

    def partition_attention(part_idx):
        query_part = queries[part_idx].astype(jnp.float32)
        key_part = keys[part_idx].astype(jnp.float32)
        value_part = values[part_idx].astype(jnp.float32)
        ids_part = batch_ids[part_idx]
        matching = ids_part[:, None] == ids_part[None, :]
        scores = jnp.einsum('qhd,khd->hqk', query_part, key_part) * scale_factor
        scores = jnp.where(matching[None], scores, -1e+30)
        highest = lax.optimization_barrier(jnp.max(scores, axis=-1, keepdims=True))
        weights = jnp.where(matching[None], jnp.exp(scores - highest), 0.0)
        weight_sum = lax.optimization_barrier(jnp.sum(weights, axis=-1))
        rounded = weights.astype(jnp.bfloat16).astype(jnp.float32)
        mixed = jnp.einsum('hqk,khd->qhd', rounded, value_part) / weight_sum.T[:, :, None]
        return mixed.reshape(GROUP, D).astype(jnp.bfloat16)
    mixed = lax.map(partition_attention, jnp.arange(PARTS_SIZE, dtype=jnp.int32)).reshape(NODES, D)
    attended = jnp.dot(mixed, w_out, preferred_element_type=jnp.float32)
    total = node_rows.astype(jnp.float32) + aggregated + attended
    spread = jnp.sqrt(lax.optimization_barrier(jnp.mean(total * total, axis=-1, keepdims=True)) + 1e-06)
    return (total / spread * norm_gain.astype(jnp.float32)).astype(jnp.bfloat16)
```

```python
import math

import jax
import jax.numpy as jnp
from jax import lax
from jax.experimental import pallas as pl
from jax.experimental.pallas import tpu as pltpu
from jax.sharding import PartitionSpec as P

MESH = pl.DeviceIdType.MESH
BF16 = jnp.bfloat16
F32 = jnp.float32
D = 512
ROWS = 512
HEADS = 8
PAIRS = 4
HEAD_DIM = 64
CAP = 32
LOOPS = 4
NX, NZ, NC = 4, 8, 2
GROUP = NX * NC
SLOTS = GROUP * CAP
KEYS = LOOPS * ROWS
QB = 256
BIG = 1e30
ORDER = (4, 3, 5, 2, 6, 1, 7, 0)


def dot(a, b):
    return jnp.dot(a, b, preferred_element_type=F32)


def dot_t(a, b):
    return lax.dot_general(a, b, (((0,), (0,)), ((), ())), preferred_element_type=F32)


def dot_nt(a, b):
    return lax.dot_general(a, b, (((1,), (1,)), ((), ())), preferred_element_type=F32)


def kernel(
    rows_hbm,
    wdst_hbm,
    wsrc_hbm,
    wval_hbm,
    wq_hbm,
    wk_hbm,
    wv_hbm,
    wout_hbm,
    gain_ref,
    send_ref,
    dstrow_ref,
    counts_ref,
    ids_ref,
    out_ref,
    rows,
    ids,
    wdst,
    wsv,
    wq,
    wk,
    wv,
    wout,
    outgoing,
    incoming,
    dsthl,
    kx,
    vx,
    qp,
    qmask,
    mixed,
    base,
    acc,
    in_sem,
    y_send,
    y_recv,
    i_send,
    i_recv,
    e_send,
    e_recv,
):
    dom = lax.axis_index("dom")
    lp = lax.axis_index("loop")
    x, z, c = dom // (NZ * NC), (dom // NC) % NZ, dom % NC

    def peer(j, i, sign):
        dx, dc = i // NC, i % NC
        px = (x + sign * dx + NX) % NX
        pz = (z + sign * j + NZ) % NZ
        pc = (c + dc) % NC
        return (px * NZ + pz) * NC + pc

    loads = [
        pltpu.make_async_copy(src, dst, in_sem.at[n])
        for n, (src, dst) in enumerate(
            [
                (rows_hbm, rows.at[0]),
                (wdst_hbm, wdst),
                (wq_hbm, wq),
                (wk_hbm, wk),
                (wv_hbm, wv),
                (wsrc_hbm, wsv.at[:, pl.ds(0, D)]),
                (wval_hbm, wsv.at[:, pl.ds(D, D)]),
                (wout_hbm, wout),
            ]
        )
    ]
    for cp in loads:
        cp.start()

    barrier = pltpu.get_barrier_semaphore()
    for k in range(1, LOOPS):
        pl.semaphore_signal(barrier, inc=1, device_id=(dom, (lp + k) % LOOPS), device_id_type=MESH)
    for j in ORDER:
        for i in range(GROUP):
            if (j, i) != (0, 0):
                pl.semaphore_signal(barrier, inc=1, device_id=(peer(j, i, 1), lp), device_id_type=MESH)

    ids[0] = ids_ref[...]
    loads[0].wait()
    row_of = lax.broadcasted_iota(jnp.int32, (ROWS, SLOTS), 0)

    copies = []
    for n, j in enumerate(ORDER):
        picks = jnp.concatenate([send_ref[pl.ds(peer(j, i, 1), 1), :] for i in range(GROUP)], axis=1)
        onehot = (row_of == picks).astype(BF16)
        picked = dot_t(onehot, rows[0]).astype(BF16)
        if j == 0:
            incoming[0, pl.ds(0, CAP), :] = picked[:CAP]
        outgoing[j] = picked
        if n == 0:
            pl.semaphore_wait(barrier, LOOPS - 1 + NX * NZ * NC - 1)
            for k in (2, 1, 3):
                to = (dom, (lp + k) % LOOPS)
                for src, dst, ss, rs in (
                    (ids.at[0], ids.at[k], i_send, i_recv),
                    (rows.at[0], rows.at[k], y_send, y_recv),
                ):
                    cp = pltpu.make_async_remote_copy(
                        src_ref=src,
                        dst_ref=dst,
                        send_sem=ss.at[k],
                        recv_sem=rs.at[k],
                        device_id=to,
                        device_id_type=MESH,
                    )
                    cp.start()
                    copies.append(cp)
        for i in range(GROUP):
            if (j, i) == (0, 0):
                continue
            cp = pltpu.make_async_remote_copy(
                src_ref=outgoing.at[j, pl.ds(i * CAP, CAP)],
                dst_ref=incoming.at[j, pl.ds(i * CAP, CAP)],
                send_sem=e_send.at[j, i],
                recv_sem=e_recv.at[j, i],
                device_id=(peer(j, i, 1), lp),
                device_id_type=MESH,
            )
            cp.start()
            copies.append(cp)
    y_copies = copies[:6]
    e_copies = copies[6:]

    loads[1].wait()
    dst_term = dot(rows[0], wdst[...])
    high = dst_term.astype(BF16)
    dsthl[:, :D] = high
    dsthl[:, D:] = (dst_term - high.astype(F32)).astype(BF16)
    loads[2].wait()
    q_all = dot(rows[0], wq[...]).astype(BF16)
    for pair in range(PAIRS):
        qp[pair] = q_all[:, pair * 128 : (pair + 1) * 128]
    loads[3].wait()
    loads[4].wait()

    def column_ids(k, b):
        line = ids[k, :, pl.ds(b * 128, 128)]
        return jnp.transpose(jnp.broadcast_to(line, (128, 128)))

    lane = lax.broadcasted_iota(jnp.int32, (128, 128), 1)
    for b in range(ROWS // 128):
        own = column_ids(0, b)
        qmask[pl.ds(b * 128, 128), :] = jnp.where((lane == own) | (lane >= 2), 0.0, -BIG).astype(BF16)

    for k in range(LOOPS):
        if k:
            for cp in y_copies:
                pass
            n = {2: 0, 1: 1, 3: 2}[k]
            y_copies[2 * n].wait_recv()
            y_copies[2 * n + 1].wait_recv()
        slab = rows[k]
        keys = dot(slab, wk[...]).astype(BF16)
        values = dot(slab, wv[...]).astype(BF16)
        for pair in range(PAIRS):
            kx[pair, pl.ds(k * ROWS, ROWS), :128] = keys[:, pair * 128 : (pair + 1) * 128]
            vx[pair, pl.ds(k * ROWS, ROWS), :128] = values[:, pair * 128 : (pair + 1) * 128]
            vx[pair, pl.ds(k * ROWS, ROWS), 128:] = jnp.ones((ROWS, 128), BF16)
        for b in range(ROWS // 128):
            hit = jnp.where(lane == column_ids(k, b), 1.0, 0.0).astype(BF16)
            for pair in range(PAIRS):
                kx[pair, pl.ds(k * ROWS + b * 128, 128), 128:] = hit

    half = lax.broadcasted_iota(jnp.int32, (QB, 128), 1) < HEAD_DIM
    exponent = math.log2(math.e) / math.sqrt(HEAD_DIM)

    def attend(step, carry):
        pair, block = step // (ROWS // QB), step % (ROWS // QB)
        at = pl.ds(pl.multiple_of(block * QB, QB), QB)
        queries = qp[pair, at, :]
        mask = qmask[at, :]
        sides = []
        for keep in (half, jnp.logical_not(half)):
            query = jnp.concatenate([jnp.where(keep, queries, 0).astype(BF16), mask], axis=1)
            scores = dot_nt(query, kx[pair])
            top = jnp.max(scores, axis=1, keepdims=True)
            weights = jnp.exp2((scores - top) * exponent).astype(BF16)
            sums = dot(weights, vx[pair])
            sides.append(sums[:, :128] / sums[:, 128:])
        mixed[pair, at, :] = jnp.where(half, sides[0], sides[1]).astype(BF16)
        return carry

    lax.fori_loop(0, PAIRS * (ROWS // QB), attend, 0)

    loads[7].wait()
    attended = rows[0].astype(F32)
    for pair in range(PAIRS):
        attended += dot(mixed[pair], wout[pl.ds(pair * 128, 128), :])
    base[...] = attended

    loads[5].wait()
    loads[6].wait()
    slot = lax.broadcasted_iota(jnp.int32, (1, CAP), 1)
    at = 0
    for n, j in enumerate(ORDER):
        for i in range(GROUP):
            if (j, i) != (0, 0):
                e_copies[at].wait_recv()
                at += 1
        lines = []
        for i in range(GROUP):
            q = peer(j, i, -1)
            lines.append(jnp.where(slot < counts_ref[0, q], dstrow_ref[pl.ds(q, 1), :], -1))
        targets = jnp.concatenate(lines, axis=1)
        onehot = (row_of == targets).astype(BF16)
        projected = dot(incoming[j], wsv[...]).astype(BF16).astype(F32)
        parts = dot_t(onehot, dsthl[...])
        gates = 0.5 + 0.5 * jnp.tanh(0.5 * (parts[:, :D] + parts[:, D:] + projected[:, :D]))
        stacked = jnp.concatenate([gates * projected[:, D:], gates], axis=1).astype(BF16)
        sums = dot(onehot, stacked)
        if n == 0:
            acc[...] = sums
        else:
            acc[...] += sums

    total = base[...] + acc[:, :D] / (1.0 + acc[:, D:])
    spread = lax.rsqrt(jnp.mean(total * total, axis=1, keepdims=True) + 1e-6)
    out_ref[...] = (total * spread * gain_ref[...]).astype(BF16)

    for cp in copies:
        cp.wait_send()


def per_device(
    node_rows,
    w_dst,
    w_src,
    w_val,
    w_query,
    w_key,
    w_value,
    w_out,
    norm_gain,
    send_rows,
    dst_rows,
    counts,
    batch_ids,
):
    hbm = pl.BlockSpec(memory_space=pl.ANY)
    vmem = pl.BlockSpec(memory_space=pltpu.VMEM)
    smem = pl.BlockSpec(memory_space=pltpu.SMEM)
    dma = pltpu.SemaphoreType.DMA
    return pl.pallas_call(
        kernel,
        out_shape=jax.ShapeDtypeStruct((ROWS, D), BF16),
        in_specs=[hbm] * 8 + [vmem] * 3 + [smem, vmem],
        out_specs=vmem,
        scratch_shapes=[
            pltpu.VMEM((LOOPS, ROWS, D), BF16),
            pltpu.VMEM((LOOPS, 1, ROWS), jnp.int32),
            pltpu.VMEM((D, D), BF16),
            pltpu.VMEM((D, 2 * D), BF16),
            pltpu.VMEM((D, D), BF16),
            pltpu.VMEM((D, D), BF16),
            pltpu.VMEM((D, D), BF16),
            pltpu.VMEM((D, D), BF16),
            pltpu.VMEM((NZ, SLOTS, D), BF16),
            pltpu.VMEM((NZ, SLOTS, D), BF16),
            pltpu.VMEM((ROWS, 2 * D), BF16),
            pltpu.VMEM((PAIRS, KEYS, 256), BF16),
            pltpu.VMEM((PAIRS, KEYS, 256), BF16),
            pltpu.VMEM((PAIRS, ROWS, 128), BF16),
            pltpu.VMEM((ROWS, 128), BF16),
            pltpu.VMEM((PAIRS, ROWS, 128), BF16),
            pltpu.VMEM((ROWS, D), F32),
            pltpu.VMEM((ROWS, 2 * D), F32),
            dma((8,)),
            dma((LOOPS,)),
            dma((LOOPS,)),
            dma((LOOPS,)),
            dma((LOOPS,)),
            dma((NZ, GROUP)),
            dma((NZ, GROUP)),
        ],
        compiler_params=pltpu.CompilerParams(
            collective_id=0, has_side_effects=True, vmem_limit_bytes=56 * 2**20
        ),
        cost_estimate=pl.CostEstimate(flops=14 * 10**9, bytes_accessed=5 * 2**20, transcendentals=9 * 10**6),
    )(
        node_rows,
        w_dst,
        w_src,
        w_val,
        w_query,
        w_key,
        w_value,
        w_out,
        norm_gain.reshape(1, D),
        send_rows.reshape(send_rows.shape[2:]),
        dst_rows.reshape(dst_rows.shape[2:]),
        counts.reshape(1, -1),
        batch_ids,
    )


def solution(mesh):
    return jax.shard_map(
        per_device,
        mesh=mesh,
        in_specs=(
            P(("dom", "loop"), None),
            P(),
            P(),
            P(),
            P(),
            P(),
            P(),
            P(),
            P(),
            P("dom", "loop", None, None),
            P("dom", "loop", None, None),
            P("dom", "loop", None),
            P("dom", "loop"),
        ),
        out_specs=P(("dom", "loop"), None),
        check_vma=False,
    )
```

```python
import math

import jax
import jax.numpy as jnp
from jax import lax
from jax.experimental import pallas as pl
from jax.experimental.pallas import tpu as pltpu
from jax.sharding import PartitionSpec as P

MESH = pl.DeviceIdType.MESH
BF16 = jnp.bfloat16
F32 = jnp.float32
D = 512
ROWS = 512
HEADS = 8
PAIRS = 4
HEAD_DIM = 64
CAP = 32
LOOPS = 4
NX, NZ, NC = 4, 8, 2
GROUP = NX * NC
PEERS = NX * NZ * NC
SLOTS = GROUP * CAP
KEYS = LOOPS * ROWS
BIG = 1e30
ORDER = (4, 3, 5, 2, 6, 1, 7, 0)
LATER = (1, 3, 2)


def dot(a, b):
    return jnp.dot(a, b, preferred_element_type=F32)


def dot_t(a, b):
    return lax.dot_general(a, b, (((0,), (0,)), ((), ())), preferred_element_type=F32)


def dot_nt(a, b):
    return lax.dot_general(a, b, (((1,), (1,)), ((), ())), preferred_element_type=F32)


def kernel(
    rows_hbm,
    wdst_hbm,
    wsrc_hbm,
    wval_hbm,
    wq_hbm,
    wk_hbm,
    wv_hbm,
    wout_hbm,
    send_hbm,
    dstrow_hbm,
    counts_hbm,
    ids_hbm,
    out_ref,
    rows,
    ids,
    send_in,
    dstrow_in,
    counts_ref,
    send_ref,
    dstrow_ref,
    wdst,
    wsv,
    wq,
    wk,
    wv,
    wout,
    outgoing,
    incoming,
    dsthl,
    hits,
    received,
    kx,
    vx,
    qp,
    qmask,
    mixed,
    base,
    acc,
    in_sem,
    y_send,
    y_recv,
    i_send,
    i_recv,
    e_send,
    e_recv,
):
    dom = lax.axis_index("dom")
    lp = lax.axis_index("loop")
    x, z, c = dom // (NZ * NC), (dom // NC) % NZ, dom % NC

    def peer(j, i, sign):
        dx, dc = i // NC, i % NC
        px = (x + sign * dx + NX) % NX
        pz = (z + sign * j + NZ) % NZ
        pc = (c + dc) % NC
        return (px * NZ + pz) * NC + pc

    loads = [
        pltpu.make_async_copy(src, dst, in_sem.at[n])
        for n, (src, dst) in enumerate(
            [
                (rows_hbm, rows.at[0]),
                (send_hbm, send_in),
                (ids_hbm, ids.at[0]),
                (dstrow_hbm, dstrow_in),
                (counts_hbm, counts_ref),
                (wdst_hbm, wdst),
                (wq_hbm, wq),
                (wk_hbm, wk),
                (wv_hbm, wv),
                (wsrc_hbm, wsv.at[:, pl.ds(0, D)]),
                (wval_hbm, wsv.at[:, pl.ds(D, D)]),
                (wout_hbm, wout),
            ]
        )
    ]
    for cp in loads[:3]:
        cp.start()

    barrier = pltpu.get_barrier_semaphore()
    for k in range(1, LOOPS):
        pl.semaphore_signal(barrier, inc=1, device_id=(dom, (lp + k) % LOOPS), device_id_type=MESH)
    for j in ORDER:
        for i in range(GROUP):
            if (j, i) != (0, 0):
                pl.semaphore_signal(barrier, inc=1, device_id=(peer(j, i, 1), lp), device_id_type=MESH)

    for cp in loads[3:]:
        cp.start()

    def by_peer(block):
        wide = jnp.concatenate([block, jnp.zeros((CAP, 128 - block.shape[1]), jnp.int32)], axis=1)
        return jnp.transpose(jnp.concatenate([wide, jnp.zeros((128 - CAP, 128), jnp.int32)], axis=0))

    loads[1].wait()
    send_ref[...] = by_peer(send_in[...])
    loads[0].wait()
    loads[2].wait()
    row_of = lax.broadcasted_iota(jnp.int32, (ROWS, SLOTS), 0)

    copies = []
    for n, j in enumerate(ORDER):
        picks = jnp.concatenate([send_ref[pl.ds(peer(j, i, 1), 1), :CAP] for i in range(GROUP)], axis=1)
        onehot = (row_of == picks).astype(BF16)
        picked = dot_t(onehot, rows[0]).astype(BF16)
        if j == 0:
            incoming[0, pl.ds(0, CAP), :] = picked[:CAP]
        outgoing[j] = picked
        if n == 0:
            pl.semaphore_wait(barrier, LOOPS - 1 + NX * NZ * NC - 1)
            for k in LATER:
                to = (dom, (lp + k) % LOOPS)
                for src, dst, ss, rs in (
                    (ids.at[0], ids.at[k], i_send, i_recv),
                    (rows.at[0], rows.at[k], y_send, y_recv),
                ):
                    cp = pltpu.make_async_remote_copy(
                        src_ref=src,
                        dst_ref=dst,
                        send_sem=ss.at[k],
                        recv_sem=rs.at[k],
                        device_id=to,
                        device_id_type=MESH,
                    )
                    cp.start()
                    copies.append(cp)
        for i in range(GROUP):
            if (j, i) == (0, 0):
                continue
            cp = pltpu.make_async_remote_copy(
                src_ref=outgoing.at[j, pl.ds(i * CAP, CAP)],
                dst_ref=incoming.at[j, pl.ds(i * CAP, CAP)],
                send_sem=e_send.at[j, i],
                recv_sem=e_recv.at[j, i],
                device_id=(peer(j, i, 1), lp),
                device_id_type=MESH,
            )
            cp.start()
            copies.append(cp)
    y_copies = copies[:6]
    e_copies = copies[6:]

    loads[5].wait()
    dst_term = dot(rows[0], wdst[...])
    high = dst_term.astype(BF16)
    dsthl[:, :D] = high
    dsthl[:, D:] = (dst_term - high.astype(F32)).astype(BF16)
    loads[6].wait()
    q_all = dot(rows[0], wq[...]).astype(BF16)
    for pair in range(PAIRS):
        qp[pair] = q_all[:, pair * 128 : (pair + 1) * 128]
    loads[7].wait()
    loads[8].wait()

    def column_ids(k, b):
        line = ids[k, :, pl.ds(b * 128, 128)]
        return jnp.transpose(jnp.broadcast_to(line, (128, 128)))

    lane = lax.broadcasted_iota(jnp.int32, (128, 128), 1)
    for b in range(ROWS // 128):
        own = column_ids(0, b)
        qmask[pl.ds(b * 128, 128), :] = jnp.where((lane == own) | (lane >= 2), 0.0, -BIG).astype(BF16)

    half = lax.broadcasted_iota(jnp.int32, (ROWS, 128), 1) < HEAD_DIM
    exponent = math.log2(math.e) / math.sqrt(HEAD_DIM)

    def project(k, place):
        to = pl.ds(place * ROWS, ROWS)
        slab = rows[k]
        hit = jnp.where(lax.broadcasted_iota(jnp.int32, (128, ROWS), 0) == ids[k], 1.0, 0.0).astype(BF16)
        keys = dot(slab, wk[...]).astype(BF16)
        values = dot(slab, wv[...]).astype(BF16)
        for pair in range(PAIRS):
            kx[pair, :128, to] = jnp.transpose(keys[:, pair * 128 : (pair + 1) * 128])
            kx[pair, 128:, to] = hit
            vx[pair, to, :128] = values[:, pair * 128 : (pair + 1) * 128]
            vx[pair, to, 128:] = jnp.ones((ROWS, 128), BF16)

    loads[3].wait()
    loads[4].wait()
    dstrow_ref[...] = by_peer(dstrow_in[...])
    slot = lax.broadcasted_iota(jnp.int32, (1, CAP), 1)

    def targets_of(j, carry):
        lines = []
        for i in range(GROUP):
            q = peer(j, i, -1)
            lines.append(jnp.where(slot < counts_ref[0, q], dstrow_ref[pl.ds(q, 1), :CAP], -1))
        onehot = (row_of == jnp.concatenate(lines, axis=1)).astype(BF16)
        hits[j] = onehot
        parts = dot_t(onehot, dsthl[...])
        received[j] = parts[:, :D] + parts[:, D:]
        return carry

    lax.fori_loop(0, NZ, targets_of, 0)
    project(0, 0)
    for n, k in enumerate(LATER):
        y_copies[2 * n].wait_recv()
        y_copies[2 * n + 1].wait_recv()
        project(k, n + 1)

    def attend(pair, carry):
        queries = qp[pair]
        sides = []
        for keep in (half, jnp.logical_not(half)):
            query = jnp.concatenate([jnp.where(keep, queries, 0).astype(BF16), qmask[...]], axis=1)
            scores = dot(query, kx[pair])
            top = jnp.max(scores, axis=1, keepdims=True)
            weights = jnp.exp2((scores - top) * exponent).astype(BF16)
            sums = dot(weights, vx[pair])
            sides.append(sums[:, :128] / sums[:, 128:])
        mixed[pair] = jnp.where(half, sides[0], sides[1]).astype(BF16)
        return carry

    lax.fori_loop(0, PAIRS, attend, 0)

    loads[11].wait()
    attended = rows[0].astype(F32)
    for pair in range(PAIRS):
        attended += dot(mixed[pair], wout[pl.ds(pair * 128, 128), :])
    base[...] = attended

    loads[9].wait()
    loads[10].wait()
    at = 0
    for n, j in enumerate(ORDER):
        for i in range(GROUP):
            if (j, i) != (0, 0):
                e_copies[at].wait_recv()
                at += 1
        projected = dot(incoming[j], wsv[...]).astype(BF16).astype(F32)
        gates = 0.5 + 0.5 * jnp.tanh(0.5 * (received[j] + projected[:, :D]))
        stacked = jnp.concatenate([gates * projected[:, D:], gates], axis=1).astype(BF16)
        sums = dot(hits[j], stacked)
        if n == 0:
            acc[...] = sums
        else:
            acc[...] += sums

    total = base[...] + acc[:, :D] / (1.0 + acc[:, D:])
    out_ref[...] = total * lax.rsqrt(jnp.mean(total * total, axis=1, keepdims=True) + 1e-6)

    for cp in copies:
        cp.wait_send()


def per_device(
    node_rows,
    w_dst,
    w_src,
    w_val,
    w_query,
    w_key,
    w_value,
    w_out,
    norm_gain,
    send_rows,
    dst_rows,
    counts,
    batch_ids,
):
    hbm = pl.BlockSpec(memory_space=pl.ANY)
    vmem = pl.BlockSpec(memory_space=pltpu.VMEM)
    dma = pltpu.SemaphoreType.DMA
    normalized = pl.pallas_call(
        kernel,
        out_shape=jax.ShapeDtypeStruct((ROWS, D), F32),
        in_specs=[hbm] * 12,
        out_specs=vmem,
        scratch_shapes=[
            pltpu.VMEM((LOOPS, ROWS, D), BF16),
            pltpu.VMEM((LOOPS, 1, ROWS), jnp.int32),
            pltpu.VMEM((CAP, PEERS), jnp.int32),
            pltpu.VMEM((CAP, PEERS), jnp.int32),
            pltpu.SMEM((1, PEERS), jnp.int32),
            pltpu.VMEM((128, 128), jnp.int32),
            pltpu.VMEM((128, 128), jnp.int32),
            pltpu.VMEM((D, D), BF16),
            pltpu.VMEM((D, 2 * D), BF16),
            pltpu.VMEM((D, D), BF16),
            pltpu.VMEM((D, D), BF16),
            pltpu.VMEM((D, D), BF16),
            pltpu.VMEM((D, D), BF16),
            pltpu.VMEM((NZ, SLOTS, D), BF16),
            pltpu.VMEM((NZ, SLOTS, D), BF16),
            pltpu.VMEM((ROWS, 2 * D), BF16),
            pltpu.VMEM((NZ, ROWS, SLOTS), BF16),
            pltpu.VMEM((NZ, SLOTS, D), F32),
            pltpu.VMEM((PAIRS, 256, KEYS), BF16),
            pltpu.VMEM((PAIRS, KEYS, 256), BF16),
            pltpu.VMEM((PAIRS, ROWS, 128), BF16),
            pltpu.VMEM((ROWS, 128), BF16),
            pltpu.VMEM((PAIRS, ROWS, 128), BF16),
            pltpu.VMEM((ROWS, D), F32),
            pltpu.VMEM((ROWS, 2 * D), F32),
            dma((12,)),
            dma((LOOPS,)),
            dma((LOOPS,)),
            dma((LOOPS,)),
            dma((LOOPS,)),
            dma((NZ, GROUP)),
            dma((NZ, GROUP)),
        ],
        compiler_params=pltpu.CompilerParams(
            collective_id=0, has_side_effects=True, vmem_limit_bytes=56 * 2**20
        ),
        cost_estimate=pl.CostEstimate(flops=14 * 10**9, bytes_accessed=5 * 2**20, transcendentals=9 * 10**6),
    )(
        node_rows,
        w_dst,
        w_src,
        w_val,
        w_query,
        w_key,
        w_value,
        w_out,
        send_rows[0, 0].T,
        dst_rows[0, 0].T,
        counts.reshape(1, -1),
        batch_ids,
    )
    return (normalized * norm_gain).astype(BF16)


def solution(mesh):
    return jax.shard_map(
        per_device,
        mesh=mesh,
        in_specs=(
            P(("dom", "loop"), None),
            P(),
            P(),
            P(),
            P(),
            P(),
            P(),
            P(),
            P(),
            P("dom", "loop", None, None),
            P("dom", "loop", None, None),
            P("dom", "loop", None),
            P("dom", "loop"),
        ),
        out_specs=P(("dom", "loop"), None),
        check_vma=False,
    )
```

```python
import math

import jax
import jax.numpy as jnp
from jax import lax
from jax.experimental import pallas as pl
from jax.experimental.pallas import tpu as pltpu
from jax.sharding import PartitionSpec as P

MESH = pl.DeviceIdType.MESH
BF16 = jnp.bfloat16
F32 = jnp.float32
D = 512
ROWS = 512
HEADS = 8
PAIRS = 4
HEAD_DIM = 64
CAP = 32
LOOPS = 4
NX, NZ, NC = 4, 8, 2
GROUP = NZ
PEERS = NX * NZ * NC
GROUPS = PEERS // GROUP
SLOTS = GROUP * CAP
KEYS = LOOPS * ROWS
BIG = 1e30
STEPS = (4, 3, 5, 2, 6, 1, 7, 0)
SELF = (1, 7)
LATER = (1, 3, 2)


def dot(a, b):
    return jnp.dot(a, b, preferred_element_type=F32)


def dot_t(a, b):
    return lax.dot_general(a, b, (((0,), (0,)), ((), ())), preferred_element_type=F32)


def dot_nt(a, b):
    return lax.dot_general(a, b, (((1,), (1,)), ((), ())), preferred_element_type=F32)


def kernel(
    rows_hbm,
    wdst_hbm,
    wsrc_hbm,
    wval_hbm,
    wq_hbm,
    wk_hbm,
    wv_hbm,
    wout_hbm,
    send_hbm,
    dstrow_hbm,
    counts_hbm,
    ids_hbm,
    gain_ref,
    out_ref,
    rows,
    ids,
    send_in,
    dstrow_in,
    counts_ref,
    send_ref,
    dstrow_ref,
    wdst,
    wsv,
    wq,
    wk,
    wv,
    wout,
    outgoing,
    incoming,
    dsthl,
    hits,
    received,
    kx,
    vx,
    qp,
    qmask,
    mixed,
    base,
    acc,
    in_sem,
    y_send,
    y_recv,
    i_send,
    i_recv,
    e_send,
    e_recv,
):
    dom = lax.axis_index("dom")
    lp = lax.axis_index("loop")
    x, z, c = dom // (NZ * NC), (dom // NC) % NZ, dom % NC

    def peer(j, i, sign):
        px = (x + sign * ((j + i) % NX) + NX) % NX
        pz = (z + sign * STEPS[i] + NZ) % NZ
        pc = (c + j // NX) % NC
        return (px * NZ + pz) * NC + pc

    loads = [
        pltpu.make_async_copy(src, dst, in_sem.at[n])
        for n, (src, dst) in enumerate(
            [
                (rows_hbm, rows.at[0]),
                (send_hbm, send_in),
                (ids_hbm, ids.at[0]),
                (dstrow_hbm, dstrow_in),
                (counts_hbm, counts_ref),
                (wdst_hbm, wdst),
                (wq_hbm, wq),
                (wk_hbm, wk),
                (wv_hbm, wv),
                (wsrc_hbm, wsv.at[:, pl.ds(0, D)]),
                (wval_hbm, wsv.at[:, pl.ds(D, D)]),
                (wout_hbm, wout),
            ]
        )
    ]
    for cp in loads[:3]:
        cp.start()

    barrier = pltpu.get_barrier_semaphore()
    for k in range(1, LOOPS):
        pl.semaphore_signal(barrier, inc=1, device_id=(dom, (lp + k) % LOOPS), device_id_type=MESH)
    for j in range(GROUPS):
        for i in range(GROUP):
            if (j, i) != SELF:
                pl.semaphore_signal(barrier, inc=1, device_id=(peer(j, i, 1), lp), device_id_type=MESH)

    for cp in loads[3:]:
        cp.start()

    def by_peer(block):
        wide = jnp.concatenate([block, jnp.zeros((CAP, 128 - block.shape[1]), jnp.int32)], axis=1)
        return jnp.transpose(jnp.concatenate([wide, jnp.zeros((128 - CAP, 128), jnp.int32)], axis=0))

    loads[1].wait()
    send_ref[...] = by_peer(send_in[...])
    loads[0].wait()
    loads[2].wait()
    row_of = lax.broadcasted_iota(jnp.int32, (ROWS, SLOTS), 0)

    copies = []
    for j in range(GROUPS):
        picks = jnp.concatenate([send_ref[pl.ds(peer(j, i, 1), 1), :CAP] for i in range(GROUP)], axis=1)
        onehot = (row_of == picks).astype(BF16)
        picked = dot_t(onehot, rows[0]).astype(BF16)
        if j == SELF[0]:
            own = pl.ds(SELF[1] * CAP, CAP)
            incoming[j, own, :] = picked[SELF[1] * CAP : (SELF[1] + 1) * CAP]
        outgoing[j] = picked
        if j == 0:
            pl.semaphore_wait(barrier, LOOPS - 1 + NX * NZ * NC - 1)
            for k in LATER:
                to = (dom, (lp + k) % LOOPS)
                for src, dst, ss, rs in (
                    (ids.at[0], ids.at[k], i_send, i_recv),
                    (rows.at[0], rows.at[k], y_send, y_recv),
                ):
                    cp = pltpu.make_async_remote_copy(
                        src_ref=src,
                        dst_ref=dst,
                        send_sem=ss.at[k],
                        recv_sem=rs.at[k],
                        device_id=to,
                        device_id_type=MESH,
                    )
                    cp.start()
                    copies.append(cp)
        for i in range(GROUP):
            if (j, i) == SELF:
                continue
            cp = pltpu.make_async_remote_copy(
                src_ref=outgoing.at[j, pl.ds(i * CAP, CAP)],
                dst_ref=incoming.at[j, pl.ds(i * CAP, CAP)],
                send_sem=e_send.at[j, i],
                recv_sem=e_recv.at[j, i],
                device_id=(peer(j, i, 1), lp),
                device_id_type=MESH,
            )
            cp.start()
            copies.append(cp)
    y_copies = copies[:6]
    e_copies = copies[6:]

    loads[5].wait()
    dst_term = dot(rows[0], wdst[...])
    high = dst_term.astype(BF16)
    dsthl[:, :D] = high
    dsthl[:, D:] = (dst_term - high.astype(F32)).astype(BF16)
    loads[6].wait()
    q_all = dot(rows[0], wq[...]).astype(BF16)
    for pair in range(PAIRS):
        qp[pair] = q_all[:, pair * 128 : (pair + 1) * 128]
    loads[7].wait()
    loads[8].wait()

    def column_ids(k, b):
        line = ids[k, :, pl.ds(b * 128, 128)]
        return jnp.transpose(jnp.broadcast_to(line, (128, 128)))

    lane = lax.broadcasted_iota(jnp.int32, (128, 128), 1)
    for b in range(ROWS // 128):
        own = column_ids(0, b)
        qmask[pl.ds(b * 128, 128), :] = jnp.where((lane == own) | (lane >= 2), 0.0, -BIG).astype(BF16)

    half = lax.broadcasted_iota(jnp.int32, (ROWS, 128), 1) < HEAD_DIM
    exponent = math.log2(math.e) / math.sqrt(HEAD_DIM)

    def project(k, place):
        to = pl.ds(place * ROWS, ROWS)
        slab = rows[k]
        hit = jnp.where(lax.broadcasted_iota(jnp.int32, (128, ROWS), 0) == ids[k], 1.0, 0.0).astype(BF16)
        keys = dot(slab, wk[...]).astype(BF16)
        values = dot(slab, wv[...]).astype(BF16)
        for pair in range(PAIRS):
            kx[pair, :128, to] = jnp.transpose(keys[:, pair * 128 : (pair + 1) * 128])
            kx[pair, 128:, to] = hit
            vx[pair, to, :128] = values[:, pair * 128 : (pair + 1) * 128]
            vx[pair, to, 128:] = jnp.ones((ROWS, 128), BF16)

    loads[3].wait()
    loads[4].wait()
    dstrow_ref[...] = by_peer(dstrow_in[...])
    slot = lax.broadcasted_iota(jnp.int32, (1, CAP), 1)

    def targets_of(j, carry):
        lines = []
        for i in range(GROUP):
            q = peer(j, i, -1)
            lines.append(jnp.where(slot < counts_ref[0, q], dstrow_ref[pl.ds(q, 1), :CAP], -1))
        onehot = (row_of == jnp.concatenate(lines, axis=1)).astype(BF16)
        hits[j] = onehot
        parts = dot_t(onehot, dsthl[...])
        received[j] = parts[:, :D] + parts[:, D:]
        return carry

    lax.fori_loop(0, GROUPS, targets_of, 0)
    project(0, 0)
    for n, k in enumerate(LATER):
        y_copies[2 * n].wait_recv()
        y_copies[2 * n + 1].wait_recv()
        project(k, n + 1)

    def attend(pair, carry):
        queries = qp[pair]
        sides = []
        for keep in (half, jnp.logical_not(half)):
            query = jnp.concatenate([jnp.where(keep, queries, 0).astype(BF16), qmask[...]], axis=1)
            scores = dot(query, kx[pair])
            top = jnp.max(scores, axis=1, keepdims=True)
            weights = jnp.exp2((scores - top) * exponent).astype(BF16)
            sums = dot(weights, vx[pair])
            sides.append(sums[:, :128] / sums[:, 128:])
        mixed[pair] = jnp.where(half, sides[0], sides[1]).astype(BF16)
        return carry

    lax.fori_loop(0, PAIRS, attend, 0)

    loads[11].wait()
    attended = rows[0].astype(F32)
    for pair in range(PAIRS):
        attended += dot(mixed[pair], wout[pl.ds(pair * 128, 128), :])
    base[...] = attended

    loads[9].wait()
    loads[10].wait()
    at = 0
    for j in range(GROUPS):
        for i in range(GROUP):
            if (j, i) != SELF:
                e_copies[at].wait_recv()
                at += 1
        projected = dot(incoming[j], wsv[...]).astype(BF16).astype(F32)
        gates = 0.5 + 0.5 * jnp.tanh(0.5 * (received[j] + projected[:, :D]))
        stacked = jnp.concatenate([gates * projected[:, D:], gates], axis=1).astype(BF16)
        sums = dot(hits[j], stacked)
        if j == 0:
            acc[...] = sums
        else:
            acc[...] += sums

    total = base[...] + acc[:, :D] / (1.0 + acc[:, D:])
    normed = total * lax.rsqrt(jnp.mean(total * total, axis=1, keepdims=True) + 1e-6)
    out_ref[...] = (normed * gain_ref[...]).astype(BF16)

    for cp in copies:
        cp.wait_send()


def per_device(
    node_rows,
    w_dst,
    w_src,
    w_val,
    w_query,
    w_key,
    w_value,
    w_out,
    norm_gain,
    send_rows,
    dst_rows,
    counts,
    batch_ids,
):
    hbm = pl.BlockSpec(memory_space=pl.ANY)
    vmem = pl.BlockSpec(memory_space=pltpu.VMEM)
    dma = pltpu.SemaphoreType.DMA
    normalized = pl.pallas_call(
        kernel,
        out_shape=jax.ShapeDtypeStruct((ROWS, D), BF16),
        in_specs=[hbm] * 12 + [vmem],
        out_specs=vmem,
        scratch_shapes=[
            pltpu.VMEM((LOOPS, ROWS, D), BF16),
            pltpu.VMEM((LOOPS, 1, ROWS), jnp.int32),
            pltpu.VMEM((CAP, PEERS), jnp.int32),
            pltpu.VMEM((CAP, PEERS), jnp.int32),
            pltpu.SMEM((1, PEERS), jnp.int32),
            pltpu.VMEM((128, 128), jnp.int32),
            pltpu.VMEM((128, 128), jnp.int32),
            pltpu.VMEM((D, D), BF16),
            pltpu.VMEM((D, 2 * D), BF16),
            pltpu.VMEM((D, D), BF16),
            pltpu.VMEM((D, D), BF16),
            pltpu.VMEM((D, D), BF16),
            pltpu.VMEM((D, D), BF16),
            pltpu.VMEM((GROUPS, SLOTS, D), BF16),
            pltpu.VMEM((GROUPS, SLOTS, D), BF16),
            pltpu.VMEM((ROWS, 2 * D), BF16),
            pltpu.VMEM((GROUPS, ROWS, SLOTS), BF16),
            pltpu.VMEM((GROUPS, SLOTS, D), F32),
            pltpu.VMEM((PAIRS, 256, KEYS), BF16),
            pltpu.VMEM((PAIRS, KEYS, 256), BF16),
            pltpu.VMEM((PAIRS, ROWS, 128), BF16),
            pltpu.VMEM((ROWS, 128), BF16),
            pltpu.VMEM((PAIRS, ROWS, 128), BF16),
            pltpu.VMEM((ROWS, D), F32),
            pltpu.VMEM((ROWS, 2 * D), F32),
            dma((12,)),
            dma((LOOPS,)),
            dma((LOOPS,)),
            dma((LOOPS,)),
            dma((LOOPS,)),
            dma((GROUPS, GROUP)),
            dma((GROUPS, GROUP)),
        ],
        compiler_params=pltpu.CompilerParams(
            collective_id=0, has_side_effects=True, vmem_limit_bytes=56 * 2**20
        ),
        cost_estimate=pl.CostEstimate(flops=14 * 10**9, bytes_accessed=5 * 2**20, transcendentals=9 * 10**6),
    )(
        node_rows,
        w_dst,
        w_src,
        w_val,
        w_query,
        w_key,
        w_value,
        w_out,
        send_rows[0, 0].T,
        dst_rows[0, 0].T,
        counts.reshape(1, -1),
        batch_ids,
        norm_gain.reshape(1, D),
    )
    return normalized


def solution(mesh):
    return jax.shard_map(
        per_device,
        mesh=mesh,
        in_specs=(
            P(("dom", "loop"), None),
            P(),
            P(),
            P(),
            P(),
            P(),
            P(),
            P(),
            P(),
            P("dom", "loop", None, None),
            P("dom", "loop", None, None),
            P("dom", "loop", None),
            P("dom", "loop"),
        ),
        out_specs=P(("dom", "loop"), None),
        check_vma=False,
    )
```
